32 devices in a mesh: rep: 2 (over y), row: 4 (over x, core), col: 4 (over z).
Axes of the slice: x: 2, y: 2, z: 4, core: 2. Of those that a mesh axis runs over, the one named last changes fastest.
Arguments:
- density: bfloat16 [8192, 4096], P(('rep', 'col'), 'row'), parts along dimension 0, may hold values from -2.5 to 2.5
- pattern: int32 [32, 16], P('rep'), parts along dimension 0, may hold values from 0 to 1, as said below
Outputs:
- product: float32 [8192, 4096], P(('rep', 'col'), 'row'), parts along dimension 0
The draws below stay inside these ranges and needn't reach their ends.
There are 2 independent parts, one for each index of `rep`. The reference program is written for one: setup_inputs(seed, part) draws one part's arguments, and reference() takes and returns one part's arrays. A program takes and returns all parts, laid end to end along the dimension named above; each array names one. Nothing has to cross between parts.
Inputs may be any that keep to these rules, and one draw needn't show every extreme that they name: `pattern`: block (a, b) is filled where b = a or b = (a + 1) mod 16. In each block row, at most 2 filled blocks lie in any aligned group of 4 block columns, and some block row reaches that bound. Block rows differ in how many blocks are filled.
All inputs are finite; a program needn't handle non-finite values.
Results may differ from the reference program's by a relative error of at most 0.0003.
Values may be sent and summed in bfloat16 or wider, within the bound.
A program may use at most 64 MiB of HBM per device.

```python
import jax
import jax.numpy as jnp
from jax import lax

BLK = 256
BROWS = 4
NBLK = 16
SLOTS = 2
ORDER = 4096
N_ROW = 4
N_COL = 4


def draw_pattern(key, part):
    key = jax.random.fold_in(key, 7)
    first, second, third = jax.random.split(key, 3)
    levels = jax.random.randint(first, (NBLK, 1), 30, 90)
    rolls = jax.random.randint(second, (NBLK, NBLK), 0, 100)
    chosen = jax.random.randint(third, (), 0, NBLK)
    rows = jnp.arange(NBLK)[:, None]
    cols = jnp.arange(NBLK)[None, :]
    band = (cols == rows) | (cols == (rows + 1) % NBLK)
    group_width = NBLK // N_ROW
    same_group = cols // group_width == rows // group_width
    forced = (rows == chosen) & same_group
    extra = ((rolls < levels) | forced) & jnp.logical_not(band)
    band_int = band.astype(jnp.int32).reshape(NBLK, N_ROW, group_width)
    extra_int = extra.astype(jnp.int32).reshape(NBLK, N_ROW, group_width)
    band_count = jnp.sum(band_int, axis=-1, keepdims=True)
    kept = extra_int * (band_count + jnp.cumsum(extra_int, axis=-1) <= SLOTS).astype(jnp.int32)
    return (band_int + kept).reshape(NBLK, NBLK).astype(jnp.int32)


def block_levels(own_key, dims, shards, smallest, largest):
    def one(dim, blocks):
        draws = jax.random.uniform(jax.random.fold_in(jax.random.fold_in(own_key, 6), dim), (blocks,), jnp.float32, smallest / len(shards), largest / len(shards))
        return jnp.repeat(jnp.exp(draws), dims[dim] // blocks).reshape((-1,) + (1,) * (len(dims) - dim - 1))

    gain = one(*shards[0])
    for cut in shards[1:]:
        gain = gain * one(*cut)
    return gain


def scatter_about(own_key, extent, deviation, most, cuts=(), held_as=jnp.bfloat16):
    loudness = block_levels(own_key, extent, cuts, -0.22, 0.18) if cuts else 1.0
    array = jax.random.normal(own_key, extent, jnp.float32) * deviation * loudness
    return jnp.minimum(jnp.maximum(array, -most), most).astype(held_as)


def setup_inputs(seed: int = 0, part: int = 0) -> dict:
    splits = jax.random.split(jax.random.key(seed), 3)
    own_keys = jax.random.split(jax.random.fold_in(splits[2], part), 3)
    return {
        "density": scatter_about(own_keys[0], (ORDER, ORDER), ((BROWS * BLK) ** -0.25), 2.5, ((0, 4), (1, 4))),
        "pattern": draw_pattern(jax.random.fold_in(jax.random.fold_in(splits[2], part), 71), part),
    }


def reference(density, pattern):
    order = density.shape[0]
    nblocks = pattern.shape[0]
    size_blk = order // nblocks
    full_mask = jnp.broadcast_to(pattern[:, None, :, None], (nblocks, size_blk, nblocks, size_blk)).reshape(order, order)
    masked = density * full_mask.astype(jnp.bfloat16)
    stripe = order // N_COL

    def one_stripe(index):
        rows = lax.dynamic_slice_in_dim(masked, index * stripe, stripe, 0)
        total = jnp.zeros((stripe, order), jnp.float32)
        for section in range(2):
            other = ((index + section) % N_COL).astype(jnp.int32)
            left = lax.dynamic_slice_in_dim(rows, other * stripe, stripe, 1)
            right = lax.dynamic_slice_in_dim(masked, other * stripe, stripe, 0)
            total = total + jnp.dot(left, right, preferred_element_type=jnp.float32)
        return total

    result = lax.map(one_stripe, jnp.arange(N_COL, dtype=jnp.int32))
    return result.reshape(order, order)
```

```python
import functools

import jax
import jax.numpy as jnp
from jax import lax
from jax.experimental import pallas as pl
from jax.experimental.pallas import tpu as pltpu
from jax.sharding import PartitionSpec as P

BLK = 256
SLOTS = 2
CORES = 2


def kernel(sizes, pat, dens, out, own, tile_a, tile_b, lhs, *rest):
    rows, cols, n_row, n_col = sizes
    panels, rest = rest[:rows], rest[rows:]
    raw, rest = rest[:rows], rest[rows:]
    raw_sem, z_send, z_recv, x_send, x_recv, fwd_send, keep_sem = rest
    tiles = (tile_a, tile_b)
    zero_at = rows * SLOTS
    chips = n_row // CORES
    ratio = cols // rows

    row, col = lax.axis_index("row"), lax.axis_index("col")
    chip, core = row // CORES, row % CORES
    sibling = chip * CORES + (CORES - 1 - core)
    below, above = (col + n_col - 1) % n_col, (col + 1) % n_col
    wanted = (col, above)
    source = [w // ratio for w in wanted]
    shift = [(w % ratio) * rows for w in wanted]

    barrier = pltpu.get_barrier_semaphore()
    for step in range(1, n_row):
        pl.semaphore_signal(barrier, inc=1, device_id={"row": (row + step) % n_row})
    pl.semaphore_signal(barrier, inc=1, device_id={"col": below})
    pl.semaphore_signal(barrier, inc=1, device_id={"col": above})

    def fetch(r):
        return pltpu.make_async_copy(dens.at[pl.ds(r * BLK, BLK)], raw[r], raw_sem.at[r])

    for r in range(rows):
        fetch(r).start()

    def column_of(block_row, device, slot):
        count, column, found = 0, 0, 0
        for c in range(cols):
            here = pat[block_row, device * cols + c]
            hit = jnp.where(count == slot, here, 0)
            column = column + hit * c
            found = found + hit
            count = count + here
        return column, found

    def slot_of(block_row, device, column):
        count, here = 0, 0
        for c in range(cols):
            value = pat[block_row, device * cols + c]
            count = count + jnp.where(c < column, value, 0)
            here = here + jnp.where(c == column, value, 0)
        return jnp.where(here == 0, -1, jnp.minimum(count, SLOTS - 1))

    def piece(ref, r):
        return ref.at[pl.ds(r * SLOTS, SLOTS)]

    def down(r):
        return pltpu.make_async_remote_copy(
            piece(own, r), panels[r].at[pl.ds(0, SLOTS)], z_send.at[r], z_recv.at[r],
            device_id={"col": below},
        )

    def spread(t, r, j):
        target = sibling if j == 0 else ((chip + j) % chips) * CORES + core
        return pltpu.make_async_remote_copy(
            piece(own, r), piece(tiles[t], r), x_send.at[t, r, j], x_recv.at[t, r],
            device_id={"row": target},
        )

    def forward(t, r):
        return pltpu.make_async_remote_copy(
            piece(tiles[t], r), piece(tiles[t], r), fwd_send.at[t, r], x_recv.at[t, r],
            device_id={"row": sibling},
        )

    def keep(t, r):
        return pltpu.make_async_copy(piece(own, r), piece(tiles[t], r), keep_sem.at[t, r])

    zero = jnp.zeros((BLK, BLK), own.dtype)
    for r in range(rows):
        fetch(r).wait()
        for s in range(SLOTS):
            block = None
            for c in range(cols):
                hit = (slot_of(col * rows + r, row, c) == s).astype(jnp.int32)
                term = raw[r][:, c * BLK : (c + 1) * BLK] * hit.astype(own.dtype)
                block = term if block is None else block + term
            own[r * SLOTS + s] = block
        if r == 0:
            pl.semaphore_wait(barrier, n_row + 1)
        down(r).start()
        for t in range(2):
            @pl.when(row == source[t])
            def _():
                for j in reversed(range(chips)):
                    spread(t, r, j).start()
                keep(t, r).start()

    own[zero_at] = zero
    tile_b[zero_at] = zero
    for r in range(rows):
        panels[r][SLOTS] = zero

    held = []
    for k in range(rows):
        slots = [slot_of(col * rows + k, row, c) for c in range(cols)]
        held.append([jnp.where(slot >= 0, k * SLOTS + slot, zero_at) for slot in slots])

    relays = [(chip != source[t] // CORES) & (core == source[t] % CORES) for t in range(2)]
    for r in range(rows):
        for t in range(2):
            @pl.when(row == source[t])
            def _():
                keep(t, r).wait()

            @pl.when(row != source[t])
            def _():
                spread(t, r, 0).wait_recv()

            @pl.when(relays[t])
            def _():
                forward(t, r).start()

        for c in range(cols):
            total = None
            for s in range(SLOTS):
                column, found = column_of(col * rows + r, source[0], s)
                at = zero_at
                for k in range(rows):
                    here = (found != 0) & (column == shift[0] + k)
                    at = jnp.where(here, held[k][c], at)
                term = jnp.dot(
                    tile_a[r * SLOTS + s], own[at], preferred_element_type=jnp.float32
                )
                total = term if total is None else total + term
            out[pl.ds(r * BLK, BLK), pl.ds(c * BLK, BLK)] = total

    for k in range(rows):
        for r in range(rows):
            slot = slot_of(col * rows + r, source[1], shift[1] + k)
            at = jnp.where(slot >= 0, r * SLOTS + slot, zero_at)
            lhs[pl.ds(r * BLK, BLK), :] = tile_b[at]
        down(k).wait_recv()

        def second_term(c, carry):
            slot = slot_of(above * rows + k, row, c)
            at = jnp.where(slot >= 0, slot, SLOTS)
            where = pl.ds(pl.multiple_of(c * BLK, BLK), BLK)
            out[:, where] += jnp.dot(
                lhs[...], panels[k][at], preferred_element_type=jnp.float32
            )
            return carry

        lax.fori_loop(0, cols, second_term, 0)

    for r in range(rows):
        down(r).wait_send()
        for t in range(2):
            @pl.when(row == source[t])
            def _():
                for j in range(chips):
                    spread(t, r, j).wait_send()

            @pl.when(relays[t])
            def _():
                forward(t, r).wait_send()


def local(density, pattern):
    stripe, width = density.shape
    rows, cols = stripe // BLK, width // BLK
    n_row, n_col = lax.axis_size("row"), lax.axis_size("col")
    chips = n_row // CORES
    dtype = density.dtype
    packed = pltpu.VMEM((rows * SLOTS + 1, BLK, BLK), dtype)
    return pl.pallas_call(
        functools.partial(kernel, (rows, cols, n_row, n_col)),
        out_shape=jax.ShapeDtypeStruct((stripe, width), jnp.float32),
        in_specs=[
            pl.BlockSpec(memory_space=pltpu.SMEM),
            pl.BlockSpec(memory_space=pl.ANY),
        ],
        out_specs=pl.BlockSpec(memory_space=pltpu.VMEM),
        scratch_shapes=[packed] * 3
        + [pltpu.VMEM((stripe, BLK), dtype)]
        + [pltpu.VMEM((SLOTS + 1, BLK, BLK), dtype)] * rows
        + [pltpu.VMEM((BLK, width), dtype)] * rows
        + [
            pltpu.SemaphoreType.DMA((rows,)),
            pltpu.SemaphoreType.DMA((rows,)),
            pltpu.SemaphoreType.DMA((rows,)),
            pltpu.SemaphoreType.DMA((2, rows, chips)),
            pltpu.SemaphoreType.DMA((2, rows)),
            pltpu.SemaphoreType.DMA((2, rows)),
            pltpu.SemaphoreType.DMA((2, rows)),
        ],
        compiler_params=pltpu.CompilerParams(
            collective_id=0, has_side_effects=True, vmem_limit_bytes=40 * 1024 * 1024
        ),
        cost_estimate=pl.CostEstimate(
            flops=4 * stripe * stripe * width,
            bytes_accessed=6 * stripe * width,
            transcendentals=0,
        ),
    )(pattern, density)


def solution(mesh):
    placed = (P(("rep", "col"), "row"), P("rep", None))
    return jax.shard_map(
        local, mesh=mesh, in_specs=placed, out_specs=P(("rep", "col"), "row"), check_vma=False
    )
```

```python
import functools

import jax
import jax.numpy as jnp
from jax import lax
from jax.experimental import pallas as pl
from jax.experimental.pallas import tpu as pltpu
from jax.sharding import PartitionSpec as P

BLK = 256
SLOTS = 2
CORES = 2


def kernel(sizes, pat_hbm, dens, out, pat, pat_sem, own, tile_a, tile_b, lhs, *rest):
    rows, cols, n_row, n_col = sizes
    panels, rest = rest[:rows], rest[rows:]
    raw, rest = rest[:rows], rest[rows:]
    raw_sem, z_send, z_recv, share_send, x_send, x_recv, fwd_send, keep_sem = rest
    tiles = (tile_a, tile_b)
    zero_at = rows * SLOTS
    chips = n_row // CORES
    ratio = cols // rows

    row, col = lax.axis_index("row"), lax.axis_index("col")
    chip, core = row // CORES, row % CORES
    sibling = chip * CORES + (CORES - 1 - core)
    below, above = (col + n_col - 1) % n_col, (col + 1) % n_col
    wanted = (col, above)
    source = [w // ratio for w in wanted]
    shift = [(w % ratio) * rows for w in wanted]

    is_source = [row == source[t] for t in range(2)]
    is_sibling = [sibling == source[t] for t in range(2)]
    is_far = [chip != source[t] // CORES for t in range(2)]

    barrier = pltpu.get_barrier_semaphore()
    for step in range(1, n_row):
        pl.semaphore_signal(barrier, inc=1, device_id={"row": (row + step) % n_row})
    pl.semaphore_signal(barrier, inc=1, device_id={"col": below})
    pl.semaphore_signal(barrier, inc=1, device_id={"col": above})

    def fetch(r):
        return pltpu.make_async_copy(dens.at[pl.ds(r * BLK, BLK)], raw[r], raw_sem.at[r])

    blocks = pltpu.make_async_copy(pat_hbm, pat, pat_sem)
    blocks.start()
    for r in range(rows):
        fetch(r).start()

    def column_of(block_row, device, slot):
        count, column, found = 0, 0, 0
        for c in range(cols):
            here = pat[block_row, device * cols + c]
            hit = jnp.where(count == slot, here, 0)
            column = column + hit * c
            found = found + hit
            count = count + here
        return column, found

    def slot_of(block_row, device, column):
        count, here = 0, 0
        for c in range(cols):
            value = pat[block_row, device * cols + c]
            count = count + jnp.where(c < column, value, 0)
            here = here + jnp.where(c == column, value, 0)
        return jnp.where(here == 0, -1, jnp.minimum(count, SLOTS - 1))

    def piece(ref, r):
        return ref.at[pl.ds(r * SLOTS, SLOTS)]

    def down(r):
        return pltpu.make_async_remote_copy(
            piece(own, r), panels[r].at[pl.ds(0, SLOTS)], z_send.at[r], z_recv.at[r],
            device_id={"col": below},
        )

    def share(t, r):
        return pltpu.make_async_remote_copy(
            piece(own, r), piece(tiles[t], r), share_send.at[t, r], x_recv.at[t, r],
            device_id={"row": sibling},
        )

    def spread(t, r, j, held):
        return pltpu.make_async_remote_copy(
            piece(held, r), piece(tiles[t], r), x_send.at[t, r, j - 1], x_recv.at[t, r],
            device_id={"row": ((chip + j) % chips) * CORES + core},
        )

    def forward(t, r):
        return pltpu.make_async_remote_copy(
            piece(tiles[t], r), piece(tiles[t], r), fwd_send.at[t, r], x_recv.at[t, r],
            device_id={"row": sibling},
        )

    def keep(t, r):
        return pltpu.make_async_copy(piece(own, r), piece(tiles[t], r), keep_sem.at[t, r])

    zero = jnp.zeros((BLK, BLK), own.dtype)
    blocks.wait()
    for r in range(rows):
        fetch(r).wait()
        for s in range(SLOTS):
            block = None
            for c in range(cols):
                hit = (slot_of(col * rows + r, row, c) == s).astype(jnp.int32)
                term = raw[r][:, c * BLK : (c + 1) * BLK] * hit.astype(own.dtype)
                block = term if block is None else block + term
            own[r * SLOTS + s] = block
        if r == 0:
            pl.semaphore_wait(barrier, n_row + 1)
        down(r).start()
        for t in (1, 0):
            @pl.when(is_source[t])
            def _():
                share(t, r).start()
                keep(t, r).start()

        @pl.when(is_source[1] & (core == r % CORES))
        def _():
            for j in range(1, chips):
                spread(1, r, j, own).start()

    for t in (1, 0):
        for r in range(rows):
            @pl.when(is_sibling[t])
            def _():
                share(t, r).wait_recv()

            @pl.when(is_sibling[t] & (core == r % CORES))
            def _():
                for j in range(1, chips):
                    spread(t, r, j, tiles[t]).start()

            if t == 0:
                @pl.when(is_source[0] & (core == r % CORES))
                def _():
                    for j in range(1, chips):
                        spread(0, r, j, own).start()

    own[zero_at] = zero
    tile_b[zero_at] = zero
    for r in range(rows):
        panels[r][SLOTS] = zero

    held = []
    for k in range(rows):
        slots = [slot_of(col * rows + k, row, c) for c in range(cols)]
        held.append([jnp.where(slot >= 0, k * SLOTS + slot, zero_at) for slot in slots])

    def relay(t, r):
        @pl.when(is_far[t] & (core == r % CORES))
        def _():
            forward(t, r).wait_recv()
            forward(t, r).start()

    def arrive(t, r):
        @pl.when(is_far[t] & (core != r % CORES))
        def _():
            forward(t, r).wait_recv()

        @pl.when(is_source[t])
        def _():
            keep(t, r).wait()

    def first_term(r):
        places = [column_of(col * rows + r, source[0], s) for s in range(SLOTS)]
        for c in range(cols):
            where = pl.ds(c * BLK, BLK)
            total = out[pl.ds(r * BLK, BLK), where]
            for s, (column, found) in enumerate(places):
                at = zero_at
                for k in range(rows):
                    here = (found != 0) & (column == shift[0] + k)
                    at = jnp.where(here, held[k][c], at)
                total = total + jnp.dot(
                    tile_a[r * SLOTS + s], own[at], preferred_element_type=jnp.float32
                )
            out[pl.ds(r * BLK, BLK), where] = total

    def second_term(k):
        for r in range(rows):
            slot = slot_of(col * rows + r, source[1], shift[1] + k)
            at = jnp.where(slot >= 0, r * SLOTS + slot, zero_at)
            lhs[pl.ds(r * BLK, BLK), :] = tile_b[at]
        ats = []
        for c in range(cols):
            slot = slot_of(above * rows + k, row, c)
            ats.append(jnp.where(slot >= 0, slot, SLOTS))
        down(k).wait_recv()
        for c, at in enumerate(ats):
            where = pl.ds(c * BLK, BLK)
            term = jnp.dot(lhs[...], panels[k][at], preferred_element_type=jnp.float32)
            out[:, where] = term if k == 0 else out[:, where] + term

    half = rows // 2
    for r in range(rows):
        relay(1, r)
    for r in range(rows):
        arrive(1, r)
    for k in range(half):
        second_term(k)
    for r in range(half):
        relay(0, r)
    for r in range(half):
        arrive(0, r)
        first_term(r)
    for k in range(half, rows):
        if k == rows - 1:
            for r in range(half, rows):
                relay(0, r)
        second_term(k)
    for r in range(half, rows):
        arrive(0, r)
        first_term(r)

    for r in range(rows):
        down(r).wait_send()
        for t in range(2):
            @pl.when(is_source[t])
            def _():
                share(t, r).wait_send()

            @pl.when(jnp.logical_not(is_far[t]) & (core == r % CORES))
            def _():
                for j in range(1, chips):
                    spread(t, r, j, own).wait_send()

            @pl.when(is_far[t] & (core == r % CORES))
            def _():
                forward(t, r).wait_send()


def local(density, pattern):
    stripe, width = density.shape
    rows, cols = stripe // BLK, width // BLK
    n_row, n_col = lax.axis_size("row"), lax.axis_size("col")
    chips = n_row // CORES
    dtype = density.dtype
    packed = pltpu.VMEM((rows * SLOTS + 1, BLK, BLK), dtype)
    return pl.pallas_call(
        functools.partial(kernel, (rows, cols, n_row, n_col)),
        out_shape=jax.ShapeDtypeStruct((stripe, width), jnp.float32),
        in_specs=[
            pl.BlockSpec(memory_space=pltpu.HBM),
            pl.BlockSpec(memory_space=pltpu.HBM),
        ],
        out_specs=pl.BlockSpec(memory_space=pltpu.VMEM),
        scratch_shapes=[pltpu.SMEM(pattern.shape, pattern.dtype), pltpu.SemaphoreType.DMA]
        + [packed] * 3
        + [pltpu.VMEM((stripe, BLK), dtype)]
        + [pltpu.VMEM((SLOTS + 1, BLK, BLK), dtype)] * rows
        + [pltpu.VMEM((BLK, width), dtype)] * rows
        + [
            pltpu.SemaphoreType.DMA((rows,)),
            pltpu.SemaphoreType.DMA((rows,)),
            pltpu.SemaphoreType.DMA((rows,)),
            pltpu.SemaphoreType.DMA((2, rows)),
            pltpu.SemaphoreType.DMA((2, rows, max(chips - 1, 1))),
            pltpu.SemaphoreType.DMA((2, rows)),
            pltpu.SemaphoreType.DMA((2, rows)),
            pltpu.SemaphoreType.DMA((2, rows)),
        ],
        compiler_params=pltpu.CompilerParams(
            collective_id=0, has_side_effects=True, vmem_limit_bytes=40 * 1024 * 1024
        ),
        cost_estimate=pl.CostEstimate(
            flops=4 * stripe * stripe * width,
            bytes_accessed=6 * stripe * width,
            transcendentals=0,
        ),
    )(pattern, density)


def solution(mesh):
    placed = (P(("rep", "col"), "row"), P("rep", None))
    return jax.shard_map(
        local, mesh=mesh, in_specs=placed, out_specs=P(("rep", "col"), "row"), check_vma=False
    )
```

```python
import functools

import jax
import jax.numpy as jnp
from jax import lax
from jax.experimental import pallas as pl
from jax.experimental.pallas import tpu as pltpu
from jax.sharding import PartitionSpec as P

BLK = 256
SLOTS = 2
CORES = 2


def kernel(sizes, pat_hbm, dens, out, pat, pat_sem, own, tile_a, tile_b, lhs, *rest):
    rows, cols, n_row, n_col = sizes
    panels, rest = rest[:rows], rest[rows:]
    raw, rest = rest[:rows], rest[rows:]
    raw_sem, z_send, z_recv, share_send, x_send, x_recv, fwd_send, keep_sem = rest
    tiles = (tile_a, tile_b)
    zero_at = rows * SLOTS
    chips = n_row // CORES
    ratio = cols // rows

    row, col = lax.axis_index("row"), lax.axis_index("col")
    chip, core = row // CORES, row % CORES
    sibling = chip * CORES + (CORES - 1 - core)
    below, above = (col + n_col - 1) % n_col, (col + 1) % n_col
    wanted = (col, above)
    source = [w // ratio for w in wanted]
    shift = [(w % ratio) * rows for w in wanted]

    is_source = [row == source[t] for t in range(2)]
    is_sibling = [sibling == source[t] for t in range(2)]
    is_far = [chip != source[t] // CORES for t in range(2)]

    barrier = pltpu.get_barrier_semaphore()
    for step in range(1, n_row):
        pl.semaphore_signal(barrier, inc=1, device_id={"row": (row + step) % n_row})
    pl.semaphore_signal(barrier, inc=1, device_id={"col": below})
    pl.semaphore_signal(barrier, inc=1, device_id={"col": above})

    def fetch(r):
        return pltpu.make_async_copy(dens.at[pl.ds(r * BLK, BLK)], raw[r], raw_sem.at[r])

    blocks = pltpu.make_async_copy(pat_hbm, pat, pat_sem)
    blocks.start()
    for r in range(rows):
        fetch(r).start()

    def column_of(block_row, device, slot):
        count, column, found = 0, 0, 0
        for c in range(cols):
            here = pat[block_row, device * cols + c]
            hit = jnp.where(count == slot, here, 0)
            column = column + hit * c
            found = found + hit
            count = count + here
        return column, found

    def slot_of(block_row, device, column):
        count, here = 0, 0
        for c in range(cols):
            value = pat[block_row, device * cols + c]
            count = count + jnp.where(c < column, value, 0)
            here = here + jnp.where(c == column, value, 0)
        return jnp.where(here == 0, -1, jnp.minimum(count, SLOTS - 1))

    def piece(ref, r):
        return ref.at[pl.ds(r * SLOTS, SLOTS)]

    def down(r):
        return pltpu.make_async_remote_copy(
            piece(own, r), panels[r].at[pl.ds(0, SLOTS)], z_send.at[r], z_recv.at[r],
            device_id={"col": below},
        )

    def share(t, r):
        return pltpu.make_async_remote_copy(
            piece(own, r), piece(tiles[t], r), share_send.at[t, r], x_recv.at[t, r],
            device_id={"row": sibling},
        )

    def spread(t, r, j, held):
        return pltpu.make_async_remote_copy(
            piece(held, r), piece(tiles[t], r), x_send.at[t, r, j - 1], x_recv.at[t, r],
            device_id={"row": ((chip + j) % chips) * CORES + core},
        )

    def forward(t, r):
        return pltpu.make_async_remote_copy(
            piece(tiles[t], r), piece(tiles[t], r), fwd_send.at[t, r], x_recv.at[t, r],
            device_id={"row": sibling},
        )

    def keep(t, r):
        return pltpu.make_async_copy(piece(own, r), piece(tiles[t], r), keep_sem.at[t, r])

    zero = jnp.zeros((BLK, BLK), own.dtype)
    blocks.wait()
    for r in range(rows):
        fetch(r).wait()
        for s in range(SLOTS):
            block = None
            for c in range(cols):
                hit = (slot_of(col * rows + r, row, c) == s).astype(jnp.int32)
                term = raw[r][:, c * BLK : (c + 1) * BLK] * hit.astype(own.dtype)
                block = term if block is None else block + term
            own[r * SLOTS + s] = block
        if r == 0:
            pl.semaphore_wait(barrier, n_row + 1)
        down(r).start()
        for t in (1, 0):
            @pl.when(is_source[t])
            def _():
                share(t, r).start()
                keep(t, r).start()

        @pl.when(is_source[1] & (core == r % CORES))
        def _():
            for j in range(1, chips):
                spread(1, r, j, own).start()

    for t in (1, 0):
        for r in range(rows):
            @pl.when(is_sibling[t])
            def _():
                share(t, r).wait_recv()

            @pl.when(is_sibling[t] & (core == r % CORES))
            def _():
                for j in range(1, chips):
                    spread(t, r, j, tiles[t]).start()

            if t == 0:
                @pl.when(is_source[0] & (core == r % CORES))
                def _():
                    for j in range(1, chips):
                        spread(0, r, j, own).start()

    own[zero_at] = zero
    tile_b[zero_at] = zero
    for r in range(rows):
        panels[r][SLOTS] = zero

    held = []
    for k in range(rows):
        slots = [slot_of(col * rows + k, row, c) for c in range(cols)]
        held.append([jnp.where(slot >= 0, k * SLOTS + slot, zero_at) for slot in slots])

    def relay(t, r):
        @pl.when(is_far[t] & (core == r % CORES))
        def _():
            forward(t, r).wait_recv()
            forward(t, r).start()

    def arrive(t, r):
        @pl.when(is_far[t] & (core != r % CORES))
        def _():
            forward(t, r).wait_recv()

        @pl.when(is_source[t])
        def _():
            keep(t, r).wait()

    def first_term(r):
        places = [column_of(col * rows + r, source[0], s) for s in range(SLOTS)]
        for c in range(cols):
            where = pl.ds(c * BLK, BLK)
            total = out[pl.ds(r * BLK, BLK), where]
            for s, (column, found) in enumerate(places):
                at = zero_at
                for k in range(rows):
                    here = (found != 0) & (column == shift[0] + k)
                    at = jnp.where(here, held[k][c], at)
                total = total + jnp.dot(
                    tile_a[r * SLOTS + s], own[at], preferred_element_type=jnp.float32
                )
            out[pl.ds(r * BLK, BLK), where] = total

    def second_term(k):
        for r in range(rows):
            slot = slot_of(col * rows + r, source[1], shift[1] + k)
            at = jnp.where(slot >= 0, r * SLOTS + slot, zero_at)
            lhs[pl.ds(r * BLK, BLK), :] = tile_b[at]
        ats = []
        for c in range(cols):
            slot = slot_of(above * rows + k, row, c)
            ats.append(jnp.where(slot >= 0, slot, SLOTS))
        down(k).wait_recv()
        for c, at in enumerate(ats):
            where = pl.ds(c * BLK, BLK)
            term = jnp.dot(lhs[...], panels[k][at], preferred_element_type=jnp.float32)
            out[:, where] = term if k == 0 else out[:, where] + term

    half = rows // 2
    for r in range(rows):
        relay(1, r)
    for r in range(rows):
        arrive(1, r)
    for k in range(half):
        second_term(k)
    for r in range(half):
        relay(0, r)
    for r in range(half):
        arrive(0, r)
        first_term(r)
    for k in range(half, rows):
        if k == rows - 1:
            for r in range(half, rows):
                relay(0, r)
        second_term(k)
    for r in range(half, rows):
        arrive(0, r)
        first_term(r)

    for r in range(rows):
        down(r).wait_send()
        for t in range(2):
            @pl.when(is_source[t])
            def _():
                share(t, r).wait_send()

            @pl.when(jnp.logical_not(is_far[t]) & (core == r % CORES))
            def _():
                for j in range(1, chips):
                    spread(t, r, j, own).wait_send()

            @pl.when(is_far[t] & (core == r % CORES))
            def _():
                forward(t, r).wait_send()


def local(density, pattern):
    stripe, width = density.shape
    rows, cols = stripe // BLK, width // BLK
    n_row, n_col = lax.axis_size("row"), lax.axis_size("col")
    chips = n_row // CORES
    dtype = density.dtype
    packed = pltpu.VMEM((rows * SLOTS + 1, BLK, BLK), dtype)
    return pl.pallas_call(
        functools.partial(kernel, (rows, cols, n_row, n_col)),
        out_shape=jax.ShapeDtypeStruct((stripe, width), jnp.float32),
        in_specs=[
            pl.BlockSpec(memory_space=pltpu.HBM),
            pl.BlockSpec(memory_space=pltpu.HBM),
        ],
        out_specs=pl.BlockSpec(memory_space=pltpu.VMEM),
        scratch_shapes=[pltpu.SMEM(pattern.shape, pattern.dtype), pltpu.SemaphoreType.DMA]
        + [packed] * 3
        + [pltpu.VMEM((stripe, BLK), dtype)]
        + [pltpu.VMEM((SLOTS + 1, BLK, BLK), dtype)] * rows
        + [pltpu.VMEM((BLK, width), dtype)] * rows
        + [
            pltpu.SemaphoreType.DMA((rows,)),
            pltpu.SemaphoreType.DMA((rows,)),
            pltpu.SemaphoreType.DMA((rows,)),
            pltpu.SemaphoreType.DMA((2, rows)),
            pltpu.SemaphoreType.DMA((2, rows, max(chips - 1, 1))),
            pltpu.SemaphoreType.DMA((2, rows)),
            pltpu.SemaphoreType.DMA((2, rows)),
            pltpu.SemaphoreType.DMA((2, rows)),
        ],
        compiler_params=pltpu.CompilerParams(
            collective_id=0, has_side_effects=True, vmem_limit_bytes=40 * 1024 * 1024
        ),
        cost_estimate=pl.CostEstimate(
            flops=4 * stripe * stripe * width,
            bytes_accessed=6 * stripe * width,
            transcendentals=0,
        ),
    )(
        pltpu.with_memory_space_constraint(pattern, pltpu.HBM),
        pltpu.with_memory_space_constraint(density, pltpu.HBM),
    )


def solution(mesh):
    placed = (P(("rep", "col"), "row"), P("rep", None))
    return jax.shard_map(
        local, mesh=mesh, in_specs=placed, out_specs=P(("rep", "col"), "row"), check_vma=False
    )
```

```python
import functools

import jax
import jax.numpy as jnp
from jax import lax
from jax.experimental import pallas as pl
from jax.experimental.pallas import tpu as pltpu
from jax.sharding import PartitionSpec as P

BLK = 256
SLOTS = 2
CORES = 2


def find_column(pat, cols, block_row, device, slot):
    count, column, found = 0, 0, 0
    for c in range(cols):
        here = pat[block_row, device * cols + c]
        hit = jnp.where(count == slot, here, 0)
        column = column + hit * c
        found = found + hit
        count = count + here
    return column, found


def find_slot(pat, cols, block_row, device, column):
    count, here = 0, 0
    for c in range(cols):
        value = pat[block_row, device * cols + c]
        count = count + jnp.where(c < column, value, 0)
        here = here + jnp.where(c == column, value, 0)
    return jnp.where(here == 0, -1, jnp.minimum(count, SLOTS - 1))


def held_at(pat, rows, cols, row, col):
    held = []
    for k in range(rows):
        slots = [find_slot(pat, cols, col * rows + k, row, c) for c in range(cols)]
        held.append([jnp.where(slot >= 0, k * SLOTS + slot, rows * SLOTS) for slot in slots])
    return held


def first_block(places, held, tile_a, own, shift, rows, r, c):
    total = None
    for s, (column, found) in enumerate(places):
        at = rows * SLOTS
        for k in range(rows):
            here = (found != 0) & (column == shift + k)
            at = jnp.where(here, held[k][c], at)
        term = jnp.dot(tile_a[r * SLOTS + s], own[at], preferred_element_type=jnp.float32)
        total = term if total is None else total + term
    return total


def finish(sizes, pat_hbm, total, own, tile_a, out, pat, pat_sem, last, sems):
    rows, cols = sizes
    half = rows // 2
    row, col = lax.axis_index("row"), lax.axis_index("col")
    ratio = cols // rows
    blocks = pltpu.make_async_copy(pat_hbm, pat, pat_sem)
    blocks.start()

    def write(r):
        ready = total.at[pl.ds(r * BLK, BLK)] if r < half else last.at[r - half]
        return pltpu.make_async_copy(ready, out.at[pl.ds(r * BLK, BLK)], sems.at[r])

    for r in range(half):
        write(r).start()
    blocks.wait()
    held = held_at(pat, rows, cols, row, col)
    for r in range(half, rows):
        places = [find_column(pat, cols, col * rows + r, col // ratio, s) for s in range(SLOTS)]
        for c in range(cols):
            where = pl.ds(c * BLK, BLK)
            block = first_block(places, held, tile_a, own, (col % ratio) * rows, rows, r, c)
            last[r - half, :, where] = total[pl.ds(r * BLK, BLK), where] + block
        write(r).start()
    for r in range(rows):
        write(r).wait()


def kernel(sizes, pat_hbm, dens, out, own, tile_a, pat, pat_sem, tile_b, lhs, *rest):
    rows, cols, n_row, n_col = sizes
    panels, rest = rest[:rows], rest[rows:]
    raw, rest = rest[:rows], rest[rows:]
    raw_sem, z_send, z_recv, share_send, x_send, x_recv, fwd_send, keep_sem = rest
    tiles = (tile_a, tile_b)
    zero_at = rows * SLOTS
    chips = n_row // CORES
    ratio = cols // rows

    row, col = lax.axis_index("row"), lax.axis_index("col")
    chip, core = row // CORES, row % CORES
    sibling = chip * CORES + (CORES - 1 - core)
    below, above = (col + n_col - 1) % n_col, (col + 1) % n_col
    wanted = (col, above)
    source = [w // ratio for w in wanted]
    shift = [(w % ratio) * rows for w in wanted]

    is_source = [row == source[t] for t in range(2)]
    is_sibling = [sibling == source[t] for t in range(2)]
    is_far = [chip != source[t] // CORES for t in range(2)]

    barrier = pltpu.get_barrier_semaphore()
    for step in range(1, n_row):
        pl.semaphore_signal(barrier, inc=1, device_id={"row": (row + step) % n_row})
    pl.semaphore_signal(barrier, inc=1, device_id={"col": below})
    pl.semaphore_signal(barrier, inc=1, device_id={"col": above})

    def turn(t, r):
        return core == (source[t] + r) % CORES

    def fetch(r):
        return pltpu.make_async_copy(dens.at[pl.ds(r * BLK, BLK)], raw[r], raw_sem.at[r])

    blocks = pltpu.make_async_copy(pat_hbm, pat, pat_sem)
    blocks.start()
    for r in range(rows):
        fetch(r).start()

    column_of = functools.partial(find_column, pat, cols)
    slot_of = functools.partial(find_slot, pat, cols)

    def piece(ref, r):
        return ref.at[pl.ds(r * SLOTS, SLOTS)]

    def down(r):
        return pltpu.make_async_remote_copy(
            piece(own, r), panels[r].at[pl.ds(0, SLOTS)], z_send.at[r], z_recv.at[r],
            device_id={"col": below},
        )

    def share(t, r):
        return pltpu.make_async_remote_copy(
            piece(own, r), piece(tiles[t], r), share_send.at[t, r], x_recv.at[t, r],
            device_id={"row": sibling},
        )

    def spread(t, r, j, held):
        return pltpu.make_async_remote_copy(
            piece(held, r), piece(tiles[t], r), x_send.at[t, r, j - 1], x_recv.at[t, r],
            device_id={"row": ((chip + j) % chips) * CORES + core},
        )

    def forward(t, r):
        return pltpu.make_async_remote_copy(
            piece(tiles[t], r), piece(tiles[t], r), fwd_send.at[t, r], x_recv.at[t, r],
            device_id={"row": sibling},
        )

    def keep(t, r):
        return pltpu.make_async_copy(piece(own, r), piece(tiles[t], r), keep_sem.at[t, r])

    zero = jnp.zeros((BLK, BLK), own.dtype)
    blocks.wait()
    for r in range(rows):
        fetch(r).wait()
        for s in range(SLOTS):
            block = None
            for c in range(cols):
                hit = (slot_of(col * rows + r, row, c) == s).astype(jnp.int32)
                term = raw[r][:, c * BLK : (c + 1) * BLK] * hit.astype(own.dtype)
                block = term if block is None else block + term
            own[r * SLOTS + s] = block
        if r == 0:
            pl.semaphore_wait(barrier, n_row + 1)
        @pl.when(is_source[1] & turn(1, r))
        def _():
            for j in range(1, chips):
                spread(1, r, j, own).start()

        down(r).start()
        for t in (1, 0):
            @pl.when(is_source[t])
            def _():
                share(t, r).start()
                keep(t, r).start()

    for t in (1, 0):
        for r in range(rows):
            @pl.when(is_sibling[t])
            def _():
                share(t, r).wait_recv()

            @pl.when(is_sibling[t] & turn(t, r))
            def _():
                for j in range(1, chips):
                    spread(t, r, j, tiles[t]).start()

            if t == 0:
                @pl.when(is_source[0] & turn(0, r))
                def _():
                    for j in range(1, chips):
                        spread(0, r, j, own).start()

    own[zero_at] = zero
    tile_b[zero_at] = zero
    for r in range(rows):
        panels[r][SLOTS] = zero

    held = held_at(pat, rows, cols, row, col)

    def relay(t, r):
        @pl.when(is_far[t] & turn(t, r))
        def _():
            forward(t, r).wait_recv()
            forward(t, r).start()

    def arrive(t, r):
        @pl.when(is_far[t] & jnp.logical_not(turn(t, r)))
        def _():
            forward(t, r).wait_recv()

        @pl.when(is_source[t])
        def _():
            keep(t, r).wait()

    def first_term(r):
        places = [column_of(col * rows + r, source[0], s) for s in range(SLOTS)]
        for c in range(cols):
            where = pl.ds(c * BLK, BLK)
            out[pl.ds(r * BLK, BLK), where] += first_block(
                places, held, tile_a, own, shift[0], rows, r, c
            )

    def second_term(k):
        for r in range(rows):
            slot = slot_of(col * rows + r, source[1], shift[1] + k)
            at = jnp.where(slot >= 0, r * SLOTS + slot, zero_at)
            lhs[pl.ds(r * BLK, BLK), :] = tile_b[at]
        ats = []
        for c in range(cols):
            slot = slot_of(above * rows + k, row, c)
            ats.append(jnp.where(slot >= 0, slot, SLOTS))
        down(k).wait_recv()
        for c, at in enumerate(ats):
            where = pl.ds(c * BLK, BLK)
            term = jnp.dot(lhs[...], panels[k][at], preferred_element_type=jnp.float32)
            out[:, where] = term if k == 0 else out[:, where] + term

    half = rows // 2
    for r in range(rows):
        relay(1, r)
    for r in range(rows):
        arrive(1, r)
    for k in range(half):
        second_term(k)
    for r in range(half):
        relay(0, r)
    for r in range(half):
        arrive(0, r)
        first_term(r)
    for k in range(half, rows):
        if k == rows - 1:
            for r in range(half, rows):
                relay(0, r)
        second_term(k)
    for r in range(half, rows):
        arrive(0, r)

    for r in range(rows):
        down(r).wait_send()
        for t in range(2):
            @pl.when(is_source[t])
            def _():
                share(t, r).wait_send()

            @pl.when(jnp.logical_not(is_far[t]) & turn(t, r))
            def _():
                for j in range(1, chips):
                    spread(t, r, j, own).wait_send()

            @pl.when(is_far[t] & turn(t, r))
            def _():
                forward(t, r).wait_send()


def local(density, pattern):
    stripe, width = density.shape
    rows, cols = stripe // BLK, width // BLK
    n_row, n_col = lax.axis_size("row"), lax.axis_size("col")
    chips = n_row // CORES
    dtype = density.dtype
    packed = pltpu.VMEM((rows * SLOTS + 1, BLK, BLK), dtype)
    kept = jax.ShapeDtypeStruct((rows * SLOTS + 1, BLK, BLK), dtype)
    result = jax.ShapeDtypeStruct((stripe, width), jnp.float32)
    pattern = pltpu.with_memory_space_constraint(pattern, pltpu.HBM)
    total, own, tile_a = pl.pallas_call(
        functools.partial(kernel, (rows, cols, n_row, n_col)),
        out_shape=(result, kept, kept),
        in_specs=[
            pl.BlockSpec(memory_space=pltpu.HBM),
            pl.BlockSpec(memory_space=pltpu.HBM),
        ],
        out_specs=[pl.BlockSpec(memory_space=pltpu.VMEM)] * 3,
        scratch_shapes=[pltpu.SMEM(pattern.shape, pattern.dtype), pltpu.SemaphoreType.DMA]
        + [packed]
        + [pltpu.VMEM((stripe, BLK), dtype)]
        + [pltpu.VMEM((SLOTS + 1, BLK, BLK), dtype)] * rows
        + [pltpu.VMEM((BLK, width), dtype)] * rows
        + [
            pltpu.SemaphoreType.DMA((rows,)),
            pltpu.SemaphoreType.DMA((rows,)),
            pltpu.SemaphoreType.DMA((rows,)),
            pltpu.SemaphoreType.DMA((2, rows)),
            pltpu.SemaphoreType.DMA((2, rows, max(chips - 1, 1))),
            pltpu.SemaphoreType.DMA((2, rows)),
            pltpu.SemaphoreType.DMA((2, rows)),
            pltpu.SemaphoreType.DMA((2, rows)),
        ],
        compiler_params=pltpu.CompilerParams(
            collective_id=0, has_side_effects=True, vmem_limit_bytes=40 * 1024 * 1024
        ),
        cost_estimate=pl.CostEstimate(
            flops=4 * stripe * stripe * width,
            bytes_accessed=6 * stripe * width,
            transcendentals=0,
        ),
    )(
        pattern,
        pltpu.with_memory_space_constraint(density, pltpu.HBM),
    )
    keep = [pltpu.with_memory_space_constraint(x, pltpu.VMEM) for x in (total, own, tile_a)]
    return pl.pallas_call(
        functools.partial(finish, (rows, cols)),
        out_shape=result,
        in_specs=[pl.BlockSpec(memory_space=pltpu.HBM)]
        + [pl.BlockSpec(memory_space=pltpu.VMEM)] * 3,
        out_specs=pl.BlockSpec(memory_space=pltpu.HBM),
        scratch_shapes=[
            pltpu.SMEM(pattern.shape, pattern.dtype),
            pltpu.SemaphoreType.DMA,
            pltpu.VMEM((rows - rows // 2, BLK, width), jnp.float32),
            pltpu.SemaphoreType.DMA((rows,)),
        ],
        compiler_params=pltpu.CompilerParams(vmem_limit_bytes=24 * 1024 * 1024),
    )(pattern, *keep)


def solution(mesh):
    placed = (P(("rep", "col"), "row"), P("rep", None))
    return jax.shard_map(
        local, mesh=mesh, in_specs=placed, out_specs=P(("rep", "col"), "row"), check_vma=False
    )
```
